32 devices in a mesh: pairs: 8 (over y, x, core), slab: 4 (over z).
Axes of the slice: x: 2, y: 2, z: 4, core: 2. Of those that a mesh axis runs over, the one named last changes fastest.
Arguments:
- amplitudes: float32 [1024, 25600], P('pairs', 'slab'), may hold values from -6 to 6
- integrals: float32 [64, 64, 25600], P('pairs', None, 'slab'), may hold values from -0.0390625 to 0.0390625
- tile_mask: int32 [16, 400], replicated, may hold values from 0 to 1, as said below
Outputs:
- residual_sym: float32 [64, 64, 1024], P('pairs', 'slab')
The draws below stay inside these ranges and needn't reach their ends.
Inputs may be any that keep to these rules, and one draw needn't show every extreme that they name: Each row of tile_mask, split into aligned runs of 100 columns, holds in every run at least 25 and at most 75 ones; in every draw some run of some row holds exactly 75.
All inputs are finite; a program needn't handle non-finite values.
Results may differ from the reference program's by a relative error of at most 0.000086.
Values sent between devices are 32-bit elements; how exact they have to be, the bound alone decides.
A program may use at most 128 MiB of HBM per device.

```python
import jax
import jax.numpy as jnp
from jax import lax

NO = 32
NV = 160
NW = 64
IJ = 1024
CD = 25600
IJT = 16
CT = 400
CT_S = 100
NZ_MAX = 75


def draw_tile_mask(key, part):
    slab_count = CT // CT_S
    count_key, spot_key, order_key = jax.random.split(key, 3)
    counts = jax.random.randint(count_key, (IJT, slab_count), CT_S // 4, NZ_MAX + 1)
    hot_spot = jax.random.randint(spot_key, (), 0, IJT * slab_count)
    flat_ids = jnp.arange(IJT * slab_count, dtype=jnp.int32).reshape(IJT, slab_count)
    counts = jnp.where(flat_ids == hot_spot, NZ_MAX, counts)
    scores = jax.random.randint(order_key, (IJT, slab_count, CT_S), 0, 1 << 20) * CT_S + jnp.arange(CT_S, dtype=jnp.int32)
    ranks = jnp.argsort(jnp.argsort(scores, axis=2), axis=2)
    return (ranks < counts[:, :, None]).astype(jnp.int32).reshape(IJT, CT)


def shard_levels(stream_key, extent, shards, smallest, high):
    def one(dim, parts):
        heights = jax.random.uniform(jax.random.fold_in(jax.random.fold_in(stream_key, 6), dim), (parts,), jnp.float32, smallest / len(shards), high / len(shards))
        return jnp.repeat(jnp.exp(heights), extent[dim] // parts).reshape((-1,) + (1,) * (len(extent) - dim - 1))

    level = one(*shards[0])
    for cut in shards[1:]:
        level = level * one(*cut)
    return level


def normal_values(rng, shape, scale, bound, pieces=(), kind=jnp.bfloat16):
    result = jax.random.normal(rng, shape, jnp.float32) * scale
    if len(pieces) > 0:
        result = shard_levels(rng, shape, pieces, -0.22, 0.18) * result
    return jnp.clip(result, min=-bound, max=bound).astype(kind)


def setup_inputs(seed: int = 0) -> dict:
    arg_keys = jax.random.split(jax.random.key(seed), 4)
    return {
        "amplitudes": normal_values(arg_keys[0], (IJ, CD), 1.0, 6.0, ((0, 8), (1, 4)), jnp.float32),
        "integrals": normal_values(arg_keys[1], (NW, NW, CD), CD ** -0.5, 0.0390625, ((0, 8), (2, 4)), jnp.float32),
        "tile_mask": draw_tile_mask(jax.random.fold_in(arg_keys[3], 71), 0),
    }


def reference(amplitudes, integrals, tile_mask):
    expanded = jnp.repeat(jnp.repeat(tile_mask.astype(jnp.float32), 64, axis=0), 64, axis=1)
    masked = amplitudes * expanded
    flat_ints = integrals.reshape(NW * NW, NV * NV)
    ladder = lax.dot_general(flat_ints, masked, (((1,), (1,)), ((), ())), precision=lax.Precision.HIGHEST, preferred_element_type=jnp.float32)
    ladder = ladder.reshape(NW, NW, NO, NO)
    residual_sym = ladder + ladder.transpose(1, 0, 3, 2)
    return residual_sym.reshape(NW, NW, NO * NO)
```

```python
import functools

import jax
import jax.numpy as jnp
from jax import lax
from jax.experimental import pallas as pl
from jax.experimental.pallas import tpu as pltpu
from jax.sharding import PartitionSpec as P

MESH = pl.DeviceIdType.MESH
NO = 32
TILE = 64
LANES = 128
PARTS = 2
F32 = jnp.float32
BF16 = jnp.bfloat16
NT = (((1,), (1,)), ((), ()))
NN = (((1,), (0,)), ((), ()))


def mirrored(source, local_a, window):
    turned = source.reshape(window, local_a, NO, NO).transpose(1, 0, 3, 2)
    return turned.reshape(local_a, window, NO * NO)


def plain_shards(amplitudes, integrals, tile_mask):
    row_count, slab_cols = amplitudes.shape
    local_a, window, _ = integrals.shape
    slab_tiles = slab_cols // TILE
    mask_slab = lax.dynamic_slice_in_dim(
        tile_mask, lax.axis_index("slab") * slab_tiles, slab_tiles, 1
    )
    row_tile = (lax.axis_index("pairs") * row_count + jnp.arange(row_count, dtype=jnp.int32)) // TILE
    flat_ints = integrals.reshape(local_a * window, slab_cols)
    local_mask = jnp.take(mask_slab, row_tile, axis=0).astype(F32)
    masked = amplitudes * jnp.repeat(local_mask, TILE, axis=1)
    partial_value = lax.dot_general(
        flat_ints,
        lax.all_gather(masked, "pairs", axis=0, tiled=True),
        NT,
        precision=lax.Precision.HIGHEST,
        preferred_element_type=F32,
    )
    total_rows = partial_value.shape[1]
    partial3 = partial_value.reshape(local_a, window, total_rows)
    swapped = lax.all_to_all(partial3, "pairs", split_axis=1, concat_axis=0, tiled=True)
    combined = partial3 + mirrored(swapped, local_a, window)
    return lax.psum_scatter(combined, "slab", scatter_dimension=1, tiled=True)


def split2(x):
    hi = x.astype(BF16)
    return hi, (x - hi.astype(F32)).astype(BF16)


def join_halves(first, second, turn_first, turn_second):
    lane = lax.broadcasted_iota(jnp.int32, first.shape, 1)
    left = lane < TILE
    straight = jnp.where(left, first, second)
    swapped = pltpu.roll(jnp.where(left, second, first), TILE, 1)
    turn = jnp.where(left, jnp.full(first.shape, turn_first), jnp.full(first.shape, turn_second))
    return jnp.where(turn == 1, swapped, straight)


def kernel(
    dims,
    pick_ref, slot_ref, amp_ref, ints_ref, out_ref,
    b0, b1, b2, b3, b4, b5, b6, b7, tiles_in, v_hi, v_lo, t_hi, t_lo, stage, part, zbuf, own, mirror, turned, perm,
    amp_sem, stage_sem, send_sem, recv_sem, z_send, z_recv, x_send, x_recv,
):
    nslab, ntile, npair, vpairs, kstep = dims
    buf = (b0, b1, b2, b3, b4, b5, b6, b7)
    pairs, slab = lax.axis_index("pairs"), lax.axis_index("slab")
    chip, core = pairs // 2, pairs % 2
    depth = npair // PARTS
    local_a, window, _ = part.shape[1:]
    band = window // nslab
    rows2 = 2 * ntile * TILE
    ab = local_a * window
    vcols = stage.shape[2]
    nstage = v_hi.shape[1] // vcols
    diagonal = slab == chip

    def flip(bits):
        got = pairs
        for bit in (1, 2, 4):
            if bits & bit:
                got = got + bit - 2 * bit * ((pairs // bit) % 2)
        return got

    peers = [lax.rem(slab + d, nslab) for d in range(1, nslab)]
    partners = [(2 * slab + h, chip) for h in range(2)]

    def fetch(i):
        return pltpu.make_async_copy(
            ints_ref.at[:, pl.ds(pl.multiple_of(i * vcols, LANES), vcols)],
            stage.at[lax.rem(i, 2)],
            stage_sem.at[lax.rem(i, 2)],
        )

    for t in range(ntile):
        def bring(v, carry, t=t):
            pltpu.make_async_copy(
                amp_ref.at[pl.ds(t * TILE, TILE), pl.ds(pl.multiple_of(v * LANES, LANES), LANES)],
                tiles_in.at[t, v],
                amp_sem.at[t],
            ).start()
            return carry

        lax.fori_loop(0, vpairs, bring, 0)
    fetch(0).start()

    barrier = pltpu.get_barrier_semaphore()
    for bits in (1, 2, 4):
        pl.semaphore_signal(barrier, inc=1, device_id=(flip(bits), slab), device_id_type=MESH)
    for peer in peers:
        pl.semaphore_signal(barrier, inc=1, device_id=(pairs, peer), device_id_type=MESH)

    @pl.when(jnp.logical_not(diagonal))
    def _():
        for partner in partners:
            pl.semaphore_signal(barrier, inc=1, device_id=partner, device_id_type=MESH)
        pl.semaphore_wait(barrier, 4 + nslab)

    @pl.when(diagonal)
    def _():
        pl.semaphore_wait(barrier, 2 + nslab)

    def send(src, dst, tile, piece, bits, lane):
        return pltpu.make_async_remote_copy(
            src_ref=buf[src].at[tile, pl.ds(piece * depth, depth)],
            dst_ref=buf[dst].at[tile, pl.ds(piece * depth, depth)],
            send_sem=send_sem.at[lane, tile, piece],
            recv_sem=recv_sem.at[dst, tile, piece],
            device_id=(flip(bits), slab),
            device_id_type=MESH,
        )

    pieces = [(t, h) for t in range(ntile) for h in range(PARTS)]
    started = []

    def go(*args):
        copy = send(*args)
        copy.start()
        started.append(copy)

    def landed(block, tile, piece):
        send(0, block, tile, piece, 1, 0).wait_recv()

    for t in range(ntile):
        pltpu.make_async_copy(tiles_in.at[t], tiles_in.at[t], amp_sem.at[t]).wait()
    for t, h in pieces:
        def pack(j, carry, t=t, h=h):
            w = h * depth + j
            joined = join_halves(
                tiles_in[t, pick_ref[0, t, 2 * w]], tiles_in[t, pick_ref[0, t, 2 * w + 1]],
                pick_ref[1, t, 2 * w], pick_ref[1, t, 2 * w + 1],
            )
            lane = lax.broadcasted_iota(jnp.int32, joined.shape, 1)
            last = jnp.full(joined.shape, w) == npair - 1
            b0[t, w] = jnp.where(jnp.logical_and(lane >= TILE, last), 0.0, joined)
            return carry

        lax.fori_loop(0, depth, pack, 0)
        go(0, 2, t, h, 2, 0)
        go(0, 4, t, h, 4, 1)
        go(0, 1, t, h, 1, 2)

    def split_ints(i, carry):
        @pl.when(i + 1 < nstage)
        def _():
            fetch(i + 1).start()

        fetch(i).wait()
        at = pl.ds(pl.multiple_of(i * vcols, LANES), vcols)
        hi, lo = split2(stage[lax.rem(i, 2)])
        v_hi[:, at] = hi
        v_lo[:, at] = lo
        return carry

    lax.fori_loop(0, nstage, split_ints, 0)

    size = perm.shape[0]

    def fill_perm(i, carry):
        at = pl.ds(pl.multiple_of(i * LANES, LANES), LANES)
        row = lax.broadcasted_iota(jnp.int32, (LANES, size), 0) + i * LANES
        col = lax.broadcasted_iota(jnp.int32, (LANES, size), 1)
        perm[at, :] = jnp.where(col == (row % NO) * NO + row // NO, 1.0, 0.0).astype(BF16)
        return carry

    lax.fori_loop(0, size // LANES, fill_perm, 0)

    def chip_of(order):
        return flip(2 * order) // 2

    def ladder(order):
        for c in range(2):
            of_core = core + c - 2 * core * c
            block = 2 * order + c
            for t in range(ntile):
                row_tile = (2 * chip_of(order) + of_core) * ntile + t
                rows = pl.ds(pl.multiple_of((of_core * ntile + t) * TILE, TILE), TILE)

                def widen(v, carry, row_tile=row_tile, block=block, rows=rows, t=t):
                    joined = join_halves(
                        buf[block][t, slot_ref[0, row_tile, 2 * v]], buf[block][t, slot_ref[0, row_tile, 2 * v + 1]],
                        slot_ref[1, row_tile, 2 * v], slot_ref[1, row_tile, 2 * v + 1],
                    )
                    hi, lo = split2(joined)
                    at = pl.ds(pl.multiple_of(v * LANES, LANES), LANES)
                    t_hi[rows, at] = hi
                    t_lo[rows, at] = lo
                    return carry

                lax.fori_loop(0, vpairs, widen, 0)

        part[order] = jnp.zeros_like(part[order])

        def multiply(k, carry):
            at = pl.ds(pl.multiple_of(k * kstep, LANES), kstep)
            dot = functools.partial(lax.dot_general, dimension_numbers=NT, preferred_element_type=F32)
            vh, vl, th, tl = v_hi[:, at], v_lo[:, at], t_hi[:, at], t_lo[:, at]
            total = dot(vh, th) + dot(vh, tl) + dot(vl, th)
            part[order] += total.reshape(local_a, window, rows2)
            return carry

        lax.fori_loop(0, t_hi.shape[1] // kstep, multiply, 0)

    def z_copy(order, d):
        return pltpu.make_async_remote_copy(
            src_ref=part.at[order, :, pl.ds(pl.multiple_of(peers[d - 1] * band, band), band)],
            dst_ref=zbuf.at[order, d - 1],
            send_sem=z_send.at[order, d - 1],
            recv_sem=z_recv.at[order, d - 1],
            device_id=(pairs, peers[d - 1]),
            device_id_type=MESH,
        )

    def give_away(order):
        for d in range(1, nslab):
            z_copy(order, d).start()

    def swap_copy(order, h):
        cols = pl.ds(pl.multiple_of(chip_of(order) * rows2, rows2), rows2)
        return pltpu.make_async_remote_copy(
            src_ref=own.at[:, pl.ds(h * local_a, local_a), cols],
            dst_ref=mirror.at[core, :, :, cols],
            send_sem=x_send.at[order, h],
            recv_sem=x_recv.at[order, core],
            device_id=partners[h],
            device_id_type=MESH,
        )

    def local_copy(order, h):
        cols = pl.ds(pl.multiple_of(chip_of(order) * rows2, rows2), rows2)
        return pltpu.make_async_copy(
            own.at[:, pl.ds(h * local_a, local_a), cols],
            mirror.at[core, :, :, cols],
            x_recv.at[order, core],
        )

    def gather_sum(order):
        for d in range(1, nslab):
            z_copy(order, d).wait_recv()
        cols = pl.ds(pl.multiple_of(chip_of(order) * rows2, rows2), rows2)
        total = part[order, :, pl.ds(pl.multiple_of(slab * band, band), band), :]
        for d in range(1, nslab):
            total = total + zbuf[order, d - 1]
        own[:, :, cols] = total
        for h in range(2):
            here = jnp.logical_and(diagonal, core == h)

            @pl.when(here)
            def _(h=h):
                local_copy(order, h).start()

            @pl.when(jnp.logical_not(here))
            def _(h=h):
                swap_copy(order, h).start()

    def ready(blocks):
        for block in blocks:
            for t, h in pieces:
                landed(block, t, h)

    ready([1])
    ladder(0)
    give_away(0)

    half = ntile // 2
    for t, h in pieces:
        landed(2, t, h)
        if t >= half:
            go(2, 6, t, h, 4, 3)
        go(2, 3, t, h, 1, 4)
        landed(4, t, h)
        if t < half:
            go(4, 6, t, h, 2, 3)
        go(4, 5, t, h, 1, 5)

    ready([3])
    ladder(1)
    give_away(1)
    gather_sum(0)
    ready([5])
    ladder(2)
    give_away(2)
    gather_sum(1)
    for t, h in pieces:
        landed(6, t, h)
        go(6, 7, t, h, 1, 6)
    ready([7])
    ladder(3)
    give_away(3)
    gather_sum(2)
    gather_sum(3)

    for order in range(4):
        for e in range(2):
            pltpu.make_async_copy(
                own.at[:, pl.ds(0, local_a), pl.ds(0, rows2)],
                mirror.at[e, :, :, pl.ds(0, rows2)],
                x_recv.at[order, e],
            ).wait()

    dot = functools.partial(lax.dot_general, dimension_numbers=NN, preferred_element_type=F32)
    for e in range(2):
        hi, lo = split2(mirror[e].reshape(local_a * local_a, size))
        turned[...] = (dot(hi, perm[...]) + dot(lo, perm[...])).reshape(local_a, local_a, size)
        at = pl.ds(e * local_a, local_a)
        for k in range(local_a):
            out_ref[k, at, :] = own[k, at, :] + turned[:, k, :]

    for copy in started:
        copy.wait_send()
    for order in range(4):
        for d in range(1, nslab):
            z_copy(order, d).wait_send()
        for h in range(2):
            @pl.when(jnp.logical_not(jnp.logical_and(diagonal, core == h)))
            def _(order=order, h=h):
                swap_copy(order, h).wait_send()


def square_shards(nslab, amplitudes, integrals, tile_mask):
    row_count, slab_cols = amplitudes.shape
    local_a, window, _ = integrals.shape
    tiles = slab_cols // TILE
    ntile = row_count // TILE
    total_rows = tile_mask.shape[0] * TILE
    most = (3 * tiles) // 4
    slots = -(-(most + 1) // (2 * PARTS)) * (2 * PARTS)
    npair = slots // 2

    mask = lax.dynamic_slice_in_dim(tile_mask, lax.axis_index("slab") * tiles, tiles, 1)
    before = jnp.triu(jnp.ones((tiles, tiles), F32), 1)
    place = jnp.dot(mask.astype(F32), before).astype(jnp.int32)
    slot = jnp.where(mask == 1, place, slots - 1)
    mine = lax.dynamic_slice_in_dim(slot, lax.axis_index("pairs") * ntile, ntile, 0)
    ids = jnp.arange(tiles, dtype=jnp.int32)
    hit = mine[:, None, :] == jnp.arange(slots, dtype=jnp.int32)[None, :, None]
    pick = jnp.max(jnp.where(hit, ids[None, None, :], 0), axis=2)

    def table(ids):
        return jnp.stack([ids // 2, (ids + jnp.arange(ids.shape[1], dtype=jnp.int32)) % 2])


    ab = local_a * window
    rows2 = 2 * row_count
    kstep = 10 * LANES
    vcols = 5 * LANES
    dims = (nslab, ntile, npair, tiles // 2, kstep)
    vmem = pl.BlockSpec(memory_space=pltpu.VMEM)
    smem = pl.BlockSpec(memory_space=pltpu.SMEM)
    band = window // nslab
    dma = pltpu.SemaphoreType.DMA
    return pl.pallas_call(
        functools.partial(kernel, dims),
        out_shape=jax.ShapeDtypeStruct((local_a, band, total_rows), F32),
        in_specs=[smem, smem] + [pl.BlockSpec(memory_space=pl.ANY)] * 2,
        out_specs=vmem,
        scratch_shapes=[
            *[pltpu.VMEM((ntile, npair, TILE, LANES), F32)] * 8,
            pltpu.VMEM((ntile, tiles // 2, TILE, LANES), F32),
            pltpu.VMEM((ab, slab_cols), BF16),
            pltpu.VMEM((ab, slab_cols), BF16),
            pltpu.VMEM((rows2, slab_cols), BF16),
            pltpu.VMEM((rows2, slab_cols), BF16),
            pltpu.VMEM((2, ab, vcols), F32),
            pltpu.VMEM((4, local_a, window, rows2), F32),
            pltpu.VMEM((4, nslab - 1, local_a, band, rows2), F32),
            pltpu.VMEM((local_a, band, total_rows), F32),
            pltpu.VMEM((2, local_a, local_a, total_rows), F32),
            pltpu.VMEM((local_a, local_a, total_rows), F32),
            pltpu.VMEM((total_rows, total_rows), BF16),
            dma((ntile,)),
            dma((2,)),
            dma((7, ntile, PARTS)),
            dma((8, ntile, PARTS)),
            dma((4, nslab - 1)),
            dma((4, nslab - 1)),
            dma((4, 2)),
            dma((4, 2)),
        ],
        compiler_params=pltpu.CompilerParams(
            collective_id=0, has_side_effects=True, vmem_limit_bytes=60 * 2**20
        ),
        cost_estimate=pl.CostEstimate(
            flops=6 * ab * total_rows * slab_cols,
            bytes_accessed=4 * (ab + row_count) * slab_cols,
            transcendentals=0,
        ),
    )(table(pick), table(slot), amplitudes, integrals.reshape(ab, slab_cols))


def solution(mesh):
    square = mesh.shape["pairs"] == 2 * mesh.shape["slab"] == 2 * 2 * 2
    body = functools.partial(square_shards, mesh.shape["slab"]) if square else plain_shards
    return jax.shard_map(
        body,
        mesh=mesh,
        in_specs=(P("pairs", "slab"), P("pairs", None, "slab"), P()),
        out_specs=P("pairs", "slab", None),
        check_vma=False,
    )
```

```python
import functools

import jax
import jax.numpy as jnp
from jax import lax
from jax.experimental import pallas as pl
from jax.experimental.pallas import tpu as pltpu
from jax.sharding import PartitionSpec as P

MESH = pl.DeviceIdType.MESH
NO = 32
TILE = 64
LANES = 128
PARTS = 2
F32 = jnp.float32
BF16 = jnp.bfloat16
NT = (((1,), (1,)), ((), ()))
NN = (((1,), (0,)), ((), ()))


def mirrored(source, local_a, window):
    turned = source.reshape(window, local_a, NO, NO).transpose(1, 0, 3, 2)
    return turned.reshape(local_a, window, NO * NO)


def plain_shards(amplitudes, integrals, tile_mask):
    row_count, slab_cols = amplitudes.shape
    local_a, window, _ = integrals.shape
    slab_tiles = slab_cols // TILE
    mask_slab = lax.dynamic_slice_in_dim(
        tile_mask, lax.axis_index("slab") * slab_tiles, slab_tiles, 1
    )
    row_tile = (lax.axis_index("pairs") * row_count + jnp.arange(row_count, dtype=jnp.int32)) // TILE
    flat_ints = integrals.reshape(local_a * window, slab_cols)
    local_mask = jnp.take(mask_slab, row_tile, axis=0).astype(F32)
    masked = amplitudes * jnp.repeat(local_mask, TILE, axis=1)
    partial_value = lax.dot_general(
        flat_ints,
        lax.all_gather(masked, "pairs", axis=0, tiled=True),
        NT,
        precision=lax.Precision.HIGHEST,
        preferred_element_type=F32,
    )
    total_rows = partial_value.shape[1]
    partial3 = partial_value.reshape(local_a, window, total_rows)
    swapped = lax.all_to_all(partial3, "pairs", split_axis=1, concat_axis=0, tiled=True)
    combined = partial3 + mirrored(swapped, local_a, window)
    return lax.psum_scatter(combined, "slab", scatter_dimension=1, tiled=True)


def split2(x):
    hi = x.astype(BF16)
    return hi, (x - hi.astype(F32)).astype(BF16)


def join_halves(first, second, turn_first, turn_second):
    lane = lax.broadcasted_iota(jnp.int32, first.shape, 1)
    left = lane < TILE
    straight = jnp.where(left, first, second)
    swapped = pltpu.roll(jnp.where(left, second, first), TILE, 1)
    turn = jnp.where(left, jnp.full(first.shape, turn_first), jnp.full(first.shape, turn_second))
    return jnp.where(turn == 1, swapped, straight)


def kernel(
    dims, pick_ref, slot_ref, amp_ref, ints_ref, out_ref, *scratch,
):
    nslab, npair, vpairs, kstep, vstep = dims
    ntile = 2
    buf = [scratch[ntile * block : ntile * (block + 1)] for block in range(8)]
    (
        tiles_in, v_hi, v_lo, t_hi, t_lo, stage, part, zbuf, group_sum, own, mirror, turned, perm,
        amp_sem, stage_sem, send_sem, recv_sem, z_send, z_recv, x_send, x_recv,
    ) = scratch[8 * ntile :]
    pairs, slab = lax.axis_index("pairs"), lax.axis_index("slab")
    chip, core = pairs // 2, pairs % 2
    depth = npair // PARTS
    local_a, window, _ = part.shape[1:]
    band = window // nslab
    rows2 = 2 * ntile * TILE
    vcols = stage.shape[2]
    nstage = v_hi.shape[1] // vcols
    diagonal = slab == chip

    def flip(bits):
        got = pairs
        for bit in (1, 2, 4):
            if bits & bit:
                got = got + bit - 2 * bit * ((pairs // bit) % 2)
        return got

    peers = [lax.rem(slab + d, nslab) for d in range(1, nslab)]
    partners = [(2 * slab + h, chip) for h in range(2)]

    def fetch(i):
        return pltpu.make_async_copy(
            ints_ref.at[:, pl.ds(pl.multiple_of(i * vcols, LANES), vcols)],
            stage.at[lax.rem(i, 2)],
            stage_sem.at[lax.rem(i, 2)],
        )

    for t in range(ntile):
        def bring(v, carry, t=t):
            pltpu.make_async_copy(
                amp_ref.at[pl.ds(t * TILE, TILE), pl.ds(pl.multiple_of(v * LANES, LANES), LANES)],
                tiles_in.at[t, v],
                amp_sem.at[t],
            ).start()
            return carry

        lax.fori_loop(0, vpairs, bring, 0)
    fetch(0).start()

    barrier = pltpu.get_barrier_semaphore()
    for bits in (1, 2, 4):
        pl.semaphore_signal(barrier, inc=1, device_id=(flip(bits), slab), device_id_type=MESH)
    for peer in peers:
        pl.semaphore_signal(barrier, inc=1, device_id=(pairs, peer), device_id_type=MESH)

    @pl.when(jnp.logical_not(diagonal))
    def _():
        for partner in partners:
            pl.semaphore_signal(barrier, inc=1, device_id=partner, device_id_type=MESH)
        pl.semaphore_wait(barrier, 4 + nslab)

    @pl.when(diagonal)
    def _():
        pl.semaphore_wait(barrier, 2 + nslab)

    def send(src, dst, tile, piece, bits, lane):
        return pltpu.make_async_remote_copy(
            src_ref=buf[src][tile].at[pl.ds(piece * depth, depth)],
            dst_ref=buf[dst][tile].at[pl.ds(piece * depth, depth)],
            send_sem=send_sem.at[lane, tile, piece],
            recv_sem=recv_sem.at[dst, tile, piece],
            device_id=(flip(bits), slab),
            device_id_type=MESH,
        )

    started = []

    def go(*args):
        copy = send(*args)
        copy.start()
        started.append(copy)

    def landed(block, tile, piece):
        send(0, block, tile, piece, 1, 0).wait_recv()

    for t in range(ntile):
        pltpu.make_async_copy(tiles_in.at[t], tiles_in.at[t], amp_sem.at[t]).wait()
    for h in range(PARTS):
        for t in range(ntile):
            def pack(j, carry, t=t, h=h):
                w = h * depth + j
                joined = join_halves(
                    tiles_in[t, pick_ref[0, t, 2 * w]], tiles_in[t, pick_ref[0, t, 2 * w + 1]],
                    pick_ref[1, t, 2 * w], pick_ref[1, t, 2 * w + 1],
                )
                lane = lax.broadcasted_iota(jnp.int32, joined.shape, 1)
                last = jnp.full(joined.shape, w) == npair - 1
                buf[0][t][w] = jnp.where(jnp.logical_and(lane >= TILE, last), 0.0, joined)
                return carry

            lax.fori_loop(0, depth, pack, 0)
            if t == 0:
                go(0, 4, t, h, 4, 1)
            else:
                go(0, 2, t, h, 2, 0)
            go(0, 1, t, h, 1, 2)

    def split_ints(i, carry):
        @pl.when(i + 1 < nstage)
        def _():
            fetch(i + 1).start()

        fetch(i).wait()
        at = pl.ds(pl.multiple_of(i * vcols, LANES), vcols)
        hi, lo = split2(stage[lax.rem(i, 2)])
        v_hi[:, at] = hi
        v_lo[:, at] = lo
        return carry

    lax.fori_loop(0, nstage, split_ints, 0)

    def chip_of(order):
        return flip(2 * order) // 2

    def widen(block, t):
        device = flip(block)
        row_tile = device * ntile + t
        rows = pl.ds(pl.multiple_of(((device % 2) * ntile + t) * TILE, TILE), TILE)
        source = buf[block][t]

        def some(i, carry):
            made = []
            for j in range(vstep):
                v = i * vstep + j
                joined = join_halves(
                    source[slot_ref[0, row_tile, 2 * v]], source[slot_ref[0, row_tile, 2 * v + 1]],
                    slot_ref[1, row_tile, 2 * v], slot_ref[1, row_tile, 2 * v + 1],
                )
                made.append(split2(joined))
            at = pl.ds(pl.multiple_of(i * (vstep * LANES), LANES), vstep * LANES)
            t_hi[rows, at] = jnp.concatenate([hi for hi, _ in made], axis=1)
            t_lo[rows, at] = jnp.concatenate([lo for _, lo in made], axis=1)
            return carry

        lax.fori_loop(0, vpairs // vstep, some, 0)

    def multiply(group):
        part[group] = jnp.zeros_like(part[group])

        def step(k, carry):
            at = pl.ds(pl.multiple_of(k * kstep, LANES), kstep)
            dot = functools.partial(lax.dot_general, dimension_numbers=NT, preferred_element_type=F32)
            vh, vl, th, tl = v_hi[:, at], v_lo[:, at], t_hi[:, at], t_lo[:, at]
            total = dot(vh, th) + dot(vh, tl) + dot(vl, th)
            part[group] += total.reshape(local_a, window, rows2)
            return carry

        lax.fori_loop(0, t_hi.shape[1] // kstep, step, 0)

    def z_copy(group, d):
        return pltpu.make_async_remote_copy(
            src_ref=part.at[group, :, pl.ds(pl.multiple_of(peers[d - 1] * band, band), band)],
            dst_ref=zbuf.at[group, d - 1],
            send_sem=z_send.at[group, d - 1],
            recv_sem=z_recv.at[group, d - 1],
            device_id=(pairs, peers[d - 1]),
            device_id_type=MESH,
        )

    def give_away(group):
        for d in range(1, nslab):
            z_copy(group, d).start()

    def slab_sum(group):
        for d in range(1, nslab):
            z_copy(group, d).wait_recv()
        total = part[group, :, pl.ds(pl.multiple_of(slab * band, band), band), :]
        for d in range(1, nslab):
            total = total + zbuf[group, d - 1]
        return total

    def columns(order):
        return pl.ds(pl.multiple_of(chip_of(order) * rows2, rows2), rows2)

    def swap_copy(order, h):
        return pltpu.make_async_remote_copy(
            src_ref=own.at[:, pl.ds(h * local_a, local_a), columns(order)],
            dst_ref=mirror.at[core, :, :, columns(order)],
            send_sem=x_send.at[order, h],
            recv_sem=x_recv.at[order, core],
            device_id=partners[h],
            device_id_type=MESH,
        )

    def swap(order):
        for h in range(2):
            here = jnp.logical_and(diagonal, core == h)

            @pl.when(here)
            def _(h=h):
                pltpu.make_async_copy(
                    own.at[:, pl.ds(h * local_a, local_a), columns(order)],
                    mirror.at[core, :, :, columns(order)],
                    x_recv.at[order, core],
                ).start()

            @pl.when(jnp.logical_not(here))
            def _(h=h):
                swap_copy(order, h).start()

    def turn(order):
        of_chip = slab
        for bit in (1, 2):
            if order & bit:
                of_chip = of_chip + bit - 2 * bit * ((slab // bit) % 2)
        theirs = pl.ds(pl.multiple_of(of_chip * rows2, rows2), rows2)
        dot = functools.partial(lax.dot_general, dimension_numbers=NN, preferred_element_type=F32)
        for e in range(2):
            pltpu.make_async_copy(
                own.at[:, pl.ds(0, local_a), theirs],
                mirror.at[e, :, :, theirs],
                x_recv.at[order, e],
            ).wait()
            hi, lo = split2(mirror[e, :, :, theirs].reshape(local_a * local_a, rows2))
            moves = perm[theirs, :]
            got = (dot(hi, moves) + dot(lo, moves)).reshape(turned.shape[1:])
            turned[e] = got if order == 0 else turned[e] + got

    for t in range(ntile):
        widen(0, t)
    for h in range(PARTS):
        go(0, 2, 0, h, 2, 0)
        go(0, 4, 1, h, 4, 1)
    for t in range(ntile):
        for h in range(PARTS):
            landed(1, t, h)
        widen(1, t)
    multiply(0)
    give_away(0)

    size = perm.shape[0]

    def fill_perm(i, carry):
        at = pl.ds(pl.multiple_of(i * LANES, LANES), LANES)
        row = lax.broadcasted_iota(jnp.int32, (LANES, size), 0) + i * LANES
        col = lax.broadcasted_iota(jnp.int32, (LANES, size), 1)
        perm[at, :] = jnp.where(col == (row % NO) * NO + row // NO, 1.0, 0.0).astype(BF16)
        return carry

    lax.fori_loop(0, size // LANES, fill_perm, 0)

    for h in range(PARTS):
        landed(2, 1, h)
        go(2, 6, 1, h, 4, 3)
        go(2, 3, 1, h, 1, 4)
        landed(4, 0, h)
        go(4, 6, 0, h, 2, 3)
        go(4, 5, 0, h, 1, 5)
    own[:, :, columns(0)] = slab_sum(0)
    swap(0)
    widen(2, 1)
    widen(4, 0)
    for h in range(PARTS):
        landed(3, 1, h)
        landed(5, 0, h)
    widen(3, 1)
    widen(5, 0)
    multiply(1)
    give_away(1)
    turn(0)

    for h in range(PARTS):
        landed(2, 0, h)
        go(2, 3, 0, h, 1, 4)
        landed(4, 1, h)
        go(4, 5, 1, h, 1, 5)
    group_sum[...] = slab_sum(1)
    widen(2, 0)
    widen(4, 1)
    for h in range(PARTS):
        landed(3, 0, h)
        landed(5, 1, h)
    widen(3, 0)
    widen(5, 1)
    multiply(2)
    give_away(2)

    for h in range(PARTS):
        for t in range(ntile):
            landed(6, t, h)
            go(6, 7, t, h, 1, 6)
    for t in range(ntile):
        widen(6, t)
    for t in range(ntile):
        for h in range(PARTS):
            landed(7, t, h)
        widen(7, t)
    multiply(3)
    give_away(3)

    early, late = group_sum[...], slab_sum(2)
    left = lax.broadcasted_iota(jnp.int32, early.shape, 2) % LANES < TILE
    own[:, :, columns(1)] = jnp.where(left, late, early)
    own[:, :, columns(2)] = jnp.where(left, early, late)
    swap(1)
    swap(2)
    own[:, :, columns(3)] = slab_sum(3)
    swap(3)
    turn(1)
    turn(2)
    turn(3)
    for e in range(2):
        at = pl.ds(e * local_a, local_a)
        for k in range(local_a):
            out_ref[k, at, :] = own[k, at, :] + turned[e, :, k, :]

    for copy in started:
        copy.wait_send()
    for order in range(4):
        for d in range(1, nslab):
            z_copy(order, d).wait_send()
        for h in range(2):
            @pl.when(jnp.logical_not(jnp.logical_and(diagonal, core == h)))
            def _(order=order, h=h):
                swap_copy(order, h).wait_send()


def square_shards(nslab, amplitudes, integrals, tile_mask):
    row_count, slab_cols = amplitudes.shape
    local_a, window, _ = integrals.shape
    tiles = slab_cols // TILE
    ntile = row_count // TILE
    total_rows = tile_mask.shape[0] * TILE
    most = (3 * tiles) // 4
    slots = -(-(most + 1) // (2 * PARTS)) * (2 * PARTS)
    npair = slots // 2

    mask = lax.dynamic_slice_in_dim(tile_mask, lax.axis_index("slab") * tiles, tiles, 1)
    before = jnp.triu(jnp.ones((tiles, tiles), F32), 1)
    place = jnp.dot(mask.astype(F32), before).astype(jnp.int32)
    slot = jnp.where(mask == 1, place, slots - 1)
    mine = lax.dynamic_slice_in_dim(slot, lax.axis_index("pairs") * ntile, ntile, 0)
    ids = jnp.arange(tiles, dtype=jnp.int32)
    hit = mine[:, None, :] == jnp.arange(slots, dtype=jnp.int32)[None, :, None]
    pick = jnp.max(jnp.where(hit, ids[None, None, :], 0), axis=2)

    def table(ids):
        return jnp.stack([ids // 2, (ids + jnp.arange(ids.shape[1], dtype=jnp.int32)) % 2])


    ab = local_a * window
    rows2 = 2 * row_count
    kstep = 10 * LANES
    vcols = 5 * LANES
    vpairs = tiles // 2
    vstep = max(n for n in range(1, 6) if vpairs % n == 0)
    dims = (nslab, npair, vpairs, kstep, vstep)
    vmem = pl.BlockSpec(memory_space=pltpu.VMEM)
    smem = pl.BlockSpec(memory_space=pltpu.SMEM)
    band = window // nslab
    dma = pltpu.SemaphoreType.DMA
    return pl.pallas_call(
        functools.partial(kernel, dims),
        out_shape=jax.ShapeDtypeStruct((local_a, band, total_rows), F32),
        in_specs=[smem, smem] + [pl.BlockSpec(memory_space=pl.ANY)] * 2,
        out_specs=vmem,
        scratch_shapes=[
            *[pltpu.VMEM((npair, TILE, LANES), F32)] * (8 * ntile),
            pltpu.VMEM((ntile, tiles // 2, TILE, LANES), F32),
            pltpu.VMEM((ab, slab_cols), BF16),
            pltpu.VMEM((ab, slab_cols), BF16),
            pltpu.VMEM((rows2, slab_cols), BF16),
            pltpu.VMEM((rows2, slab_cols), BF16),
            pltpu.VMEM((2, ab, vcols), F32),
            pltpu.VMEM((4, local_a, window, rows2), F32),
            pltpu.VMEM((4, nslab - 1, local_a, band, rows2), F32),
            pltpu.VMEM((local_a, band, rows2), F32),
            pltpu.VMEM((local_a, band, total_rows), F32),
            pltpu.VMEM((2, local_a, local_a, total_rows), F32),
            pltpu.VMEM((2, local_a, local_a, total_rows), F32),
            pltpu.VMEM((total_rows, total_rows), BF16),
            dma((ntile,)),
            dma((2,)),
            dma((7, ntile, PARTS)),
            dma((8, ntile, PARTS)),
            dma((4, nslab - 1)),
            dma((4, nslab - 1)),
            dma((4, 2)),
            dma((4, 2)),
        ],
        compiler_params=pltpu.CompilerParams(
            collective_id=0, has_side_effects=True, vmem_limit_bytes=60 * 2**20
        ),
        cost_estimate=pl.CostEstimate(
            flops=6 * ab * total_rows * slab_cols,
            bytes_accessed=4 * (ab + row_count) * slab_cols,
            transcendentals=0,
        ),
    )(table(pick), table(slot), amplitudes, integrals.reshape(ab, slab_cols))


def solution(mesh):
    square = mesh.shape["pairs"] == 2 * mesh.shape["slab"] == 2 * 2 * 2
    body = functools.partial(square_shards, mesh.shape["slab"]) if square else plain_shards
    return jax.shard_map(
        body,
        mesh=mesh,
        in_specs=(P("pairs", "slab"), P("pairs", None, "slab"), P()),
        out_specs=P("pairs", "slab", None),
        check_vma=False,
    )
```

```python
import functools

import jax
import jax.numpy as jnp
from jax import lax
from jax.experimental import pallas as pl
from jax.experimental.pallas import tpu as pltpu
from jax.sharding import PartitionSpec as P

MESH = pl.DeviceIdType.MESH
NO = 32
TILE = 64
LANES = 128
PARTS = 2
F32 = jnp.float32
BF16 = jnp.bfloat16
NT = (((1,), (1,)), ((), ()))
NN = (((1,), (0,)), ((), ()))


def mirrored(source, local_a, window):
    turned = source.reshape(window, local_a, NO, NO).transpose(1, 0, 3, 2)
    return turned.reshape(local_a, window, NO * NO)


def plain_shards(amplitudes, integrals, tile_mask):
    row_count, slab_cols = amplitudes.shape
    local_a, window, _ = integrals.shape
    slab_tiles = slab_cols // TILE
    mask_slab = lax.dynamic_slice_in_dim(
        tile_mask, lax.axis_index("slab") * slab_tiles, slab_tiles, 1
    )
    row_tile = (lax.axis_index("pairs") * row_count + jnp.arange(row_count, dtype=jnp.int32)) // TILE
    flat_ints = integrals.reshape(local_a * window, slab_cols)
    local_mask = jnp.take(mask_slab, row_tile, axis=0).astype(F32)
    masked = amplitudes * jnp.repeat(local_mask, TILE, axis=1)
    partial_value = lax.dot_general(
        flat_ints,
        lax.all_gather(masked, "pairs", axis=0, tiled=True),
        NT,
        precision=lax.Precision.HIGHEST,
        preferred_element_type=F32,
    )
    total_rows = partial_value.shape[1]
    partial3 = partial_value.reshape(local_a, window, total_rows)
    swapped = lax.all_to_all(partial3, "pairs", split_axis=1, concat_axis=0, tiled=True)
    combined = partial3 + mirrored(swapped, local_a, window)
    return lax.psum_scatter(combined, "slab", scatter_dimension=1, tiled=True)


def split2(x):
    hi = x.astype(BF16)
    return hi, (x - hi.astype(F32)).astype(BF16)


def join_halves(first, second, turn_first, turn_second):
    lane = lax.broadcasted_iota(jnp.int32, first.shape, 1)
    left = lane < TILE
    straight = jnp.where(left, first, second)
    swapped = pltpu.roll(jnp.where(left, second, first), TILE, 1)
    turn = jnp.where(left, jnp.full(first.shape, turn_first), jnp.full(first.shape, turn_second))
    return jnp.where(turn == 1, swapped, straight)


def kernel(
    dims, pick_ref, slot_ref, amp_ref, ints_ref, out_ref, *scratch,
):
    nslab, npair, vpairs, kstep, vstep = dims
    ntile = 2
    buf = [scratch[ntile * block : ntile * (block + 1)] for block in range(8)]
    (
        tiles_in, v_hi, v_lo, t_hi, t_lo, stage, part, zbuf, group_sum, own, mirror, turned, perm,
        amp_sem, stage_sem, send_sem, recv_sem, z_send, z_recv, x_send, x_recv,
    ) = scratch[8 * ntile :]
    pairs, slab = lax.axis_index("pairs"), lax.axis_index("slab")
    chip, core = pairs // 2, pairs % 2
    depth = npair // PARTS
    local_a, window, _ = part.shape[1:]
    band = window // nslab
    rows2 = 2 * ntile * TILE
    vcols = stage.shape[2]
    nstage = v_hi.shape[1] // vcols
    diagonal = slab == chip

    def flip(bits):
        got = pairs
        for bit in (1, 2, 4):
            if bits & bit:
                got = got + bit - 2 * bit * ((pairs // bit) % 2)
        return got

    peers = [lax.rem(slab + d, nslab) for d in range(1, nslab)]
    partners = [(2 * slab + h, chip) for h in range(2)]

    def fetch(i):
        return pltpu.make_async_copy(
            ints_ref.at[:, pl.ds(pl.multiple_of(i * vcols, LANES), vcols)],
            stage.at[lax.rem(i, 2)],
            stage_sem.at[lax.rem(i, 2)],
        )

    for t in range(ntile):
        def bring(v, carry, t=t):
            pltpu.make_async_copy(
                amp_ref.at[pl.ds(t * TILE, TILE), pl.ds(pl.multiple_of(v * LANES, LANES), LANES)],
                tiles_in.at[t, v],
                amp_sem.at[t],
            ).start()
            return carry

        lax.fori_loop(0, vpairs, bring, 0)
    fetch(0).start()

    barrier = pltpu.get_barrier_semaphore()
    for bits in (1, 2, 4):
        pl.semaphore_signal(barrier, inc=1, device_id=(flip(bits), slab), device_id_type=MESH)
    for peer in peers:
        pl.semaphore_signal(barrier, inc=1, device_id=(pairs, peer), device_id_type=MESH)

    @pl.when(jnp.logical_not(diagonal))
    def _():
        for partner in partners:
            pl.semaphore_signal(barrier, inc=1, device_id=partner, device_id_type=MESH)
        pl.semaphore_wait(barrier, 4 + nslab)

    @pl.when(diagonal)
    def _():
        pl.semaphore_wait(barrier, 2 + nslab)

    def send(src, dst, tile, piece, bits, lane):
        return pltpu.make_async_remote_copy(
            src_ref=buf[src][tile].at[pl.ds(piece * depth, depth)],
            dst_ref=buf[dst][tile].at[pl.ds(piece * depth, depth)],
            send_sem=send_sem.at[lane, tile, piece],
            recv_sem=recv_sem.at[dst, tile, piece],
            device_id=(flip(bits), slab),
            device_id_type=MESH,
        )

    started = []

    def go(*args):
        copy = send(*args)
        copy.start()
        started.append(copy)

    def landed(block, tile, piece):
        send(0, block, tile, piece, 1, 0).wait_recv()

    for t in range(ntile):
        pltpu.make_async_copy(tiles_in.at[t], tiles_in.at[t], amp_sem.at[t]).wait()
    for h in range(PARTS):
        for t in range(ntile):
            def pack(j, carry, t=t, h=h):
                w = h * depth + j
                joined = join_halves(
                    tiles_in[t, pick_ref[0, t, 2 * w]], tiles_in[t, pick_ref[0, t, 2 * w + 1]],
                    pick_ref[1, t, 2 * w], pick_ref[1, t, 2 * w + 1],
                )
                lane = lax.broadcasted_iota(jnp.int32, joined.shape, 1)
                last = jnp.full(joined.shape, w) == npair - 1
                buf[0][t][w] = jnp.where(jnp.logical_and(lane >= TILE, last), 0.0, joined)
                return carry

            lax.fori_loop(0, depth, pack, 0)
            if t == 0:
                go(0, 4, t, h, 4, 1)
            else:
                go(0, 2, t, h, 2, 0)
            go(0, 1, t, h, 1, 2)

    def split_ints(i, carry):
        @pl.when(i + 1 < nstage)
        def _():
            fetch(i + 1).start()

        fetch(i).wait()
        at = pl.ds(pl.multiple_of(i * vcols, LANES), vcols)
        hi, lo = split2(stage[lax.rem(i, 2)])
        v_hi[:, at] = hi
        v_lo[:, at] = lo
        return carry

    lax.fori_loop(0, nstage, split_ints, 0)

    def chip_of(order):
        return flip(2 * order) // 2

    def widen(block, t, by_tile=False):
        device = flip(block)
        row_tile = device * ntile + t
        spot = 2 * t + device % 2 if by_tile else (device % 2) * ntile + t
        rows = pl.ds(pl.multiple_of(spot * TILE, TILE), TILE)
        source = buf[block][t]

        def some(i, carry):
            made = []
            for j in range(vstep):
                v = i * vstep + j
                joined = join_halves(
                    source[slot_ref[0, row_tile, 2 * v]], source[slot_ref[0, row_tile, 2 * v + 1]],
                    slot_ref[1, row_tile, 2 * v], slot_ref[1, row_tile, 2 * v + 1],
                )
                made.append(split2(joined))
            at = pl.ds(pl.multiple_of(i * (vstep * LANES), LANES), vstep * LANES)
            t_hi[rows, at] = jnp.concatenate([hi for hi, _ in made], axis=1)
            t_lo[rows, at] = jnp.concatenate([lo for _, lo in made], axis=1)
            return carry

        lax.fori_loop(0, vpairs // vstep, some, 0)

    def extent(group):
        if group < 3:
            return group, pl.ds(0, rows2)
        return 3, pl.ds((group - 3) * LANES, LANES)

    def multiply(group):
        at_part, rows = extent(group)
        part[at_part, :, :, rows] = jnp.zeros((local_a, window, rows.size), F32)

        def step(k, carry):
            at = pl.ds(pl.multiple_of(k * kstep, LANES), kstep)
            dot = functools.partial(lax.dot_general, dimension_numbers=NT, preferred_element_type=F32)
            vh, vl, th, tl = v_hi[:, at], v_lo[:, at], t_hi[rows, at], t_lo[rows, at]
            total = dot(vh, th) + dot(vh, tl) + dot(vl, th)
            part[at_part, :, :, rows] += total.reshape(local_a, window, rows.size)
            return carry

        lax.fori_loop(0, t_hi.shape[1] // kstep, step, 0)

    def z_copy(group, d):
        at_part, rows = extent(group)
        return pltpu.make_async_remote_copy(
            src_ref=part.at[at_part, :, pl.ds(pl.multiple_of(peers[d - 1] * band, band), band), rows],
            dst_ref=zbuf.at[at_part, d - 1, :, :, rows],
            send_sem=z_send.at[group, d - 1],
            recv_sem=z_recv.at[group, d - 1],
            device_id=(pairs, peers[d - 1]),
            device_id_type=MESH,
        )

    def give_away(group):
        for d in range(1, nslab):
            z_copy(group, d).start()

    def slab_sum(group):
        at_part, rows = extent(group)
        for d in range(1, nslab):
            z_copy(group, d).wait_recv()
        total = part[at_part, :, pl.ds(pl.multiple_of(slab * band, band), band), rows]
        for d in range(1, nslab):
            total = total + zbuf[at_part, d - 1, :, :, rows]
        return total

    def columns(order):
        return pl.ds(pl.multiple_of(chip_of(order) * rows2, rows2), rows2)

    def swap_copy(order, h):
        return pltpu.make_async_remote_copy(
            src_ref=own.at[:, pl.ds(h * local_a, local_a), columns(order)],
            dst_ref=mirror.at[core, :, :, columns(order)],
            send_sem=x_send.at[order, h],
            recv_sem=x_recv.at[order, core],
            device_id=partners[h],
            device_id_type=MESH,
        )

    def swap(order):
        for h in range(2):
            here = jnp.logical_and(diagonal, core == h)

            @pl.when(here)
            def _(h=h):
                pltpu.make_async_copy(
                    own.at[:, pl.ds(h * local_a, local_a), columns(order)],
                    mirror.at[core, :, :, columns(order)],
                    x_recv.at[order, core],
                ).start()

            @pl.when(jnp.logical_not(here))
            def _(h=h):
                swap_copy(order, h).start()

    def turn(order):
        of_chip = slab
        for bit in (1, 2):
            if order & bit:
                of_chip = of_chip + bit - 2 * bit * ((slab // bit) % 2)
        theirs = pl.ds(pl.multiple_of(of_chip * rows2, rows2), rows2)
        dot = functools.partial(lax.dot_general, dimension_numbers=NN, preferred_element_type=F32)
        for e in range(2):
            pltpu.make_async_copy(
                own.at[:, pl.ds(0, local_a), theirs],
                mirror.at[e, :, :, theirs],
                x_recv.at[order, e],
            ).wait()
            hi, lo = split2(mirror[e, :, :, theirs].reshape(local_a * local_a, rows2))
            moves = perm[theirs, :]
            got = (dot(hi, moves) + dot(lo, moves)).reshape(turned.shape[1:])
            turned[e] = got if order == 0 else turned[e] + got

    for t in range(ntile):
        widen(0, t)
    for h in range(PARTS):
        go(0, 2, 0, PARTS - 1 - h, 2, 0)
        go(0, 4, 1, h, 4, 1)
    for t in range(ntile):
        for h in range(PARTS):
            landed(1, t, h)
        widen(1, t)
    multiply(0)
    give_away(0)

    size = perm.shape[0]

    def fill_perm(i, carry):
        at = pl.ds(pl.multiple_of(i * LANES, LANES), LANES)
        row = lax.broadcasted_iota(jnp.int32, (LANES, size), 0) + i * LANES
        col = lax.broadcasted_iota(jnp.int32, (LANES, size), 1)
        perm[at, :] = jnp.where(col == (row % NO) * NO + row // NO, 1.0, 0.0).astype(BF16)
        return carry

    lax.fori_loop(0, size // LANES, fill_perm, 0)

    for h in range(PARTS):
        landed(4, 0, h)
        if h == 0:
            go(4, 6, 0, h, 2, 3)
        go(4, 5, 0, h, 1, 5)
        landed(2, 1, h)
        go(2, 3, 1, h, 1, 4)
    own[:, :, columns(0)] = slab_sum(0)
    swap(0)
    widen(2, 1)
    widen(4, 0)
    for h in range(PARTS):
        landed(3, 1, h)
        landed(5, 0, h)
    widen(3, 1)
    widen(5, 0)
    multiply(1)
    give_away(1)
    turn(0)

    for h in range(PARTS):
        back = PARTS - 1 - h
        landed(2, 0, back)
        if h == 0:
            go(2, 6, 0, back, 4, 3)
            go(2, 6, 1, back, 4, 3)
        go(2, 3, 0, back, 1, 4)
        landed(4, 1, h)
        if h == 0:
            go(4, 6, 1, h, 2, 3)
        go(4, 5, 1, h, 1, 5)
    group_sum[...] = slab_sum(1)
    widen(2, 0)
    widen(4, 1)
    for h in range(PARTS):
        landed(3, 0, h)
        landed(5, 1, h)
    widen(3, 0)
    widen(5, 1)
    multiply(2)
    give_away(2)

    for t in range(ntile):
        for h in range(PARTS):
            landed(6, t, h)
            go(6, 7, t, h, 1, 6)
        widen(6, t, True)
        for h in range(PARTS):
            landed(7, t, h)
        widen(7, t, True)
        multiply(3 + t)
        give_away(3 + t)

    early, late = group_sum[...], slab_sum(2)
    left = lax.broadcasted_iota(jnp.int32, early.shape, 2) % LANES < TILE
    own[:, :, columns(1)] = jnp.where(left, late, early)
    own[:, :, columns(2)] = jnp.where(left, early, late)
    swap(1)
    swap(2)
    turn(1)
    turn(2)
    zero, one = slab_sum(3), slab_sum(4)
    left = lax.broadcasted_iota(jnp.int32, zero.shape, 2) < TILE
    front = jnp.where(left, zero, pltpu.roll(one, TILE, 2))
    back = jnp.where(left, pltpu.roll(zero, TILE, 2), one)
    own[:, :, columns(3)] = jnp.concatenate([front, back], axis=2)
    swap(3)
    turn(3)
    for e in range(2):
        at = pl.ds(e * local_a, local_a)
        for k in range(local_a):
            out_ref[k, at, :] = own[k, at, :] + turned[e, :, k, :]

    for copy in started:
        copy.wait_send()
    for group in range(5):
        for d in range(1, nslab):
            z_copy(group, d).wait_send()
    for order in range(4):
        for h in range(2):
            @pl.when(jnp.logical_not(jnp.logical_and(diagonal, core == h)))
            def _(order=order, h=h):
                swap_copy(order, h).wait_send()


def square_shards(nslab, amplitudes, integrals, tile_mask):
    row_count, slab_cols = amplitudes.shape
    local_a, window, _ = integrals.shape
    tiles = slab_cols // TILE
    ntile = row_count // TILE
    total_rows = tile_mask.shape[0] * TILE
    most = (3 * tiles) // 4
    slots = -(-(most + 1) // (2 * PARTS)) * (2 * PARTS)
    npair = slots // 2

    mask = lax.dynamic_slice_in_dim(tile_mask, lax.axis_index("slab") * tiles, tiles, 1)
    before = jnp.triu(jnp.ones((tiles, tiles), F32), 1)
    place = jnp.dot(mask.astype(F32), before).astype(jnp.int32)
    slot = jnp.where(mask == 1, place, slots - 1)
    mine = lax.dynamic_slice_in_dim(slot, lax.axis_index("pairs") * ntile, ntile, 0)
    ids = jnp.arange(tiles, dtype=jnp.int32)
    hit = mine[:, None, :] == jnp.arange(slots, dtype=jnp.int32)[None, :, None]
    pick = jnp.max(jnp.where(hit, ids[None, None, :], 0), axis=2)

    def table(ids):
        return jnp.stack([ids // 2, (ids + jnp.arange(ids.shape[1], dtype=jnp.int32)) % 2])


    ab = local_a * window
    rows2 = 2 * row_count
    kstep = 10 * LANES
    vcols = 5 * LANES
    vpairs = tiles // 2
    vstep = max(n for n in range(1, 6) if vpairs % n == 0)
    dims = (nslab, npair, vpairs, kstep, vstep)
    vmem = pl.BlockSpec(memory_space=pltpu.VMEM)
    smem = pl.BlockSpec(memory_space=pltpu.SMEM)
    band = window // nslab
    dma = pltpu.SemaphoreType.DMA
    return pl.pallas_call(
        functools.partial(kernel, dims),
        out_shape=jax.ShapeDtypeStruct((local_a, band, total_rows), F32),
        in_specs=[smem, smem] + [pl.BlockSpec(memory_space=pl.ANY)] * 2,
        out_specs=vmem,
        scratch_shapes=[
            *[pltpu.VMEM((npair, TILE, LANES), F32)] * (8 * ntile),
            pltpu.VMEM((ntile, tiles // 2, TILE, LANES), F32),
            pltpu.VMEM((ab, slab_cols), BF16),
            pltpu.VMEM((ab, slab_cols), BF16),
            pltpu.VMEM((rows2, slab_cols), BF16),
            pltpu.VMEM((rows2, slab_cols), BF16),
            pltpu.VMEM((2, ab, vcols), F32),
            pltpu.VMEM((4, local_a, window, rows2), F32),
            pltpu.VMEM((4, nslab - 1, local_a, band, rows2), F32),
            pltpu.VMEM((local_a, band, rows2), F32),
            pltpu.VMEM((local_a, band, total_rows), F32),
            pltpu.VMEM((2, local_a, local_a, total_rows), F32),
            pltpu.VMEM((2, local_a, local_a, total_rows), F32),
            pltpu.VMEM((total_rows, total_rows), BF16),
            dma((ntile,)),
            dma((2,)),
            dma((7, ntile, PARTS)),
            dma((8, ntile, PARTS)),
            dma((5, nslab - 1)),
            dma((5, nslab - 1)),
            dma((4, 2)),
            dma((4, 2)),
        ],
        compiler_params=pltpu.CompilerParams(
            collective_id=0, has_side_effects=True, vmem_limit_bytes=60 * 2**20
        ),
        cost_estimate=pl.CostEstimate(
            flops=6 * ab * total_rows * slab_cols,
            bytes_accessed=4 * (ab + row_count) * slab_cols,
            transcendentals=0,
        ),
    )(table(pick), table(slot), amplitudes, integrals.reshape(ab, slab_cols))


def solution(mesh):
    square = mesh.shape["pairs"] == 2 * mesh.shape["slab"] == 2 * 2 * 2
    body = functools.partial(square_shards, mesh.shape["slab"]) if square else plain_shards
    return jax.shard_map(
        body,
        mesh=mesh,
        in_specs=(P("pairs", "slab"), P("pairs", None, "slab"), P()),
        out_specs=P("pairs", "slab", None),
        check_vma=False,
    )
```

```python
import functools

import jax
import jax.numpy as jnp
from jax import lax
from jax.experimental import pallas as pl
from jax.experimental.pallas import tpu as pltpu
from jax.sharding import PartitionSpec as P

MESH = pl.DeviceIdType.MESH
NO = 32
TILE = 64
LANES = 128
PARTS = 2
F32 = jnp.float32
BF16 = jnp.bfloat16
NT = (((1,), (1,)), ((), ()))
NN = (((1,), (0,)), ((), ()))


def mirrored(source, local_a, window):
    turned = source.reshape(window, local_a, NO, NO).transpose(1, 0, 3, 2)
    return turned.reshape(local_a, window, NO * NO)


def plain_shards(amplitudes, integrals, tile_mask):
    row_count, slab_cols = amplitudes.shape
    local_a, window, _ = integrals.shape
    slab_tiles = slab_cols // TILE
    mask_slab = lax.dynamic_slice_in_dim(
        tile_mask, lax.axis_index("slab") * slab_tiles, slab_tiles, 1
    )
    row_tile = (lax.axis_index("pairs") * row_count + jnp.arange(row_count, dtype=jnp.int32)) // TILE
    flat_ints = integrals.reshape(local_a * window, slab_cols)
    local_mask = jnp.take(mask_slab, row_tile, axis=0).astype(F32)
    masked = amplitudes * jnp.repeat(local_mask, TILE, axis=1)
    partial_value = lax.dot_general(
        flat_ints,
        lax.all_gather(masked, "pairs", axis=0, tiled=True),
        NT,
        precision=lax.Precision.HIGHEST,
        preferred_element_type=F32,
    )
    total_rows = partial_value.shape[1]
    partial3 = partial_value.reshape(local_a, window, total_rows)
    swapped = lax.all_to_all(partial3, "pairs", split_axis=1, concat_axis=0, tiled=True)
    combined = partial3 + mirrored(swapped, local_a, window)
    return lax.psum_scatter(combined, "slab", scatter_dimension=1, tiled=True)


def split2(x):
    hi = x.astype(BF16)
    return hi, (x - hi.astype(F32)).astype(BF16)


def join_halves(first, second, turn_first, turn_second):
    lane = lax.broadcasted_iota(jnp.int32, first.shape, 1)
    left = lane < TILE
    straight = jnp.where(left, first, second)
    swapped = pltpu.roll(jnp.where(left, second, first), TILE, 1)
    turn = jnp.where(left, jnp.full(first.shape, turn_first), jnp.full(first.shape, turn_second))
    return jnp.where(turn == 1, swapped, straight)


def kernel(
    dims, pick_ref, pick_turn, slot_ref, slot_turn, amp_ref, ints_ref, out_ref, *scratch,
):
    nslab, npair, vpairs, kstep, vstep = dims
    ntile = 2
    buf = [scratch[ntile * block : ntile * (block + 1)] for block in range(8)]
    (
        tiles_in, v_hi, v_lo, t_hi, t_lo, stage, part, zbuf, group_sum, own, mirror, turned, perm,
        amp_sem, stage_sem, send_sem, recv_sem, z_send, z_recv, x_send, x_recv,
    ) = scratch[8 * ntile :]
    pairs, slab = lax.axis_index("pairs"), lax.axis_index("slab")
    chip, core = pairs // 2, pairs % 2
    depth = npair // PARTS
    local_a, window, _ = part.shape[1:]
    band = window // nslab
    rows2 = 2 * ntile * TILE
    vcols = stage.shape[2]
    nstage = v_hi.shape[1] // vcols
    diagonal = slab == chip

    def flip(bits):
        got = pairs
        for bit in (1, 2, 4):
            if bits & bit:
                got = got + bit - 2 * bit * ((pairs // bit) % 2)
        return got

    peers = [lax.rem(slab + d, nslab) for d in range(1, nslab)]
    partners = [(2 * slab + h, chip) for h in range(2)]

    def fetch(i):
        return pltpu.make_async_copy(
            ints_ref.at[:, pl.ds(pl.multiple_of(i * vcols, LANES), vcols)],
            stage.at[lax.rem(i, 2)],
            stage_sem.at[lax.rem(i, 2)],
        )

    for t in range(ntile):
        def bring(v, carry, t=t):
            pltpu.make_async_copy(
                amp_ref.at[pl.ds(t * TILE, TILE), pl.ds(pl.multiple_of(v * LANES, LANES), LANES)],
                tiles_in.at[t, v],
                amp_sem.at[t],
            ).start()
            return carry

        lax.fori_loop(0, vpairs, bring, 0)
    fetch(0).start()

    barrier = pltpu.get_barrier_semaphore()
    for bits in (1, 2, 4):
        pl.semaphore_signal(barrier, inc=1, device_id=(flip(bits), slab), device_id_type=MESH)
    for peer in peers:
        pl.semaphore_signal(barrier, inc=1, device_id=(pairs, peer), device_id_type=MESH)

    @pl.when(jnp.logical_not(diagonal))
    def _():
        for partner in partners:
            pl.semaphore_signal(barrier, inc=1, device_id=partner, device_id_type=MESH)
        pl.semaphore_wait(barrier, 4 + nslab)

    @pl.when(diagonal)
    def _():
        pl.semaphore_wait(barrier, 2 + nslab)

    def send(src, dst, tile, piece, bits, lane):
        return pltpu.make_async_remote_copy(
            src_ref=buf[src][tile].at[pl.ds(piece * depth, depth)],
            dst_ref=buf[dst][tile].at[pl.ds(piece * depth, depth)],
            send_sem=send_sem.at[lane, tile, piece],
            recv_sem=recv_sem.at[dst, tile, piece],
            device_id=(flip(bits), slab),
            device_id_type=MESH,
        )

    started = []

    def go(*args):
        copy = send(*args)
        copy.start()
        started.append(copy)

    def landed(block, tile, piece):
        send(0, block, tile, piece, 1, 0).wait_recv()

    for t in range(ntile):
        pltpu.make_async_copy(tiles_in.at[t], tiles_in.at[t], amp_sem.at[t]).wait()
    for h in range(PARTS):
        for t in range(ntile):
            def pack(j, carry, t=t, h=h):
                w = h * depth + j
                joined = join_halves(
                    tiles_in[t, pick_ref[t, 2 * w]], tiles_in[t, pick_ref[t, 2 * w + 1]],
                    pick_turn[t, 2 * w], pick_turn[t, 2 * w + 1],
                )
                lane = lax.broadcasted_iota(jnp.int32, joined.shape, 1)
                last = jnp.full(joined.shape, w) == npair - 1
                buf[0][t][w] = jnp.where(jnp.logical_and(lane >= TILE, last), 0.0, joined)
                return carry

            lax.fori_loop(0, depth, pack, 0)
            if t == 0:
                go(0, 4, t, h, 4, 1)
            else:
                go(0, 2, t, h, 2, 0)
            go(0, 1, t, h, 1, 2)

    def split_ints(i, carry):
        @pl.when(i + 1 < nstage)
        def _():
            fetch(i + 1).start()

        fetch(i).wait()
        at = pl.ds(pl.multiple_of(i * vcols, LANES), vcols)
        hi, lo = split2(stage[lax.rem(i, 2)])
        v_hi[:, at] = hi
        v_lo[:, at] = lo
        return carry

    lax.fori_loop(0, nstage, split_ints, 0)

    def chip_of(order):
        return flip(2 * order) // 2

    def widen(block, t, by_tile=False):
        device = flip(block)
        row_tile = device * ntile + t
        spot = 2 * t + device % 2 if by_tile else (device % 2) * ntile + t
        rows = pl.ds(pl.multiple_of(spot * TILE, TILE), TILE)
        source = buf[block][t]

        def some(i, carry):
            made = []
            for j in range(vstep):
                v = i * vstep + j
                joined = join_halves(
                    source[slot_ref[row_tile, 2 * v]], source[slot_ref[row_tile, 2 * v + 1]],
                    slot_turn[row_tile, 2 * v], slot_turn[row_tile, 2 * v + 1],
                )
                made.append(split2(joined))
            at = pl.ds(pl.multiple_of(i * (vstep * LANES), LANES), vstep * LANES)
            t_hi[rows, at] = jnp.concatenate([hi for hi, _ in made], axis=1)
            t_lo[rows, at] = jnp.concatenate([lo for _, lo in made], axis=1)
            return carry

        lax.fori_loop(0, vpairs // vstep, some, 0)

    def extent(group):
        if group < 3:
            return group, pl.ds(0, rows2)
        return 3, pl.ds((group - 3) * LANES, LANES)

    def multiply(group):
        at_part, rows = extent(group)
        part[at_part, :, :, rows] = jnp.zeros((local_a, window, rows.size), F32)

        def step(k, carry):
            at = pl.ds(pl.multiple_of(k * kstep, LANES), kstep)
            dot = functools.partial(lax.dot_general, dimension_numbers=NT, preferred_element_type=F32)
            vh, vl, th, tl = v_hi[:, at], v_lo[:, at], t_hi[rows, at], t_lo[rows, at]
            total = dot(vh, th) + dot(vh, tl) + dot(vl, th)
            part[at_part, :, :, rows] += total.reshape(local_a, window, rows.size)
            return carry

        lax.fori_loop(0, t_hi.shape[1] // kstep, step, 0)

    def z_copy(group, d):
        at_part, rows = extent(group)
        return pltpu.make_async_remote_copy(
            src_ref=part.at[at_part, :, pl.ds(pl.multiple_of(peers[d - 1] * band, band), band), rows],
            dst_ref=zbuf.at[at_part, d - 1, :, :, rows],
            send_sem=z_send.at[group, d - 1],
            recv_sem=z_recv.at[group, d - 1],
            device_id=(pairs, peers[d - 1]),
            device_id_type=MESH,
        )

    def give_away(group):
        for d in range(1, nslab):
            z_copy(group, d).start()

    def slab_sum(group):
        at_part, rows = extent(group)
        for d in range(1, nslab):
            z_copy(group, d).wait_recv()
        total = part[at_part, :, pl.ds(pl.multiple_of(slab * band, band), band), rows]
        for d in range(1, nslab):
            total = total + zbuf[at_part, d - 1, :, :, rows]
        return total

    def columns(order):
        return pl.ds(pl.multiple_of(chip_of(order) * rows2, rows2), rows2)

    def swap_copy(order, h):
        return pltpu.make_async_remote_copy(
            src_ref=own.at[:, pl.ds(h * local_a, local_a), columns(order)],
            dst_ref=mirror.at[core, :, :, columns(order)],
            send_sem=x_send.at[order, h],
            recv_sem=x_recv.at[order, core],
            device_id=partners[h],
            device_id_type=MESH,
        )

    def swap(order):
        for h in range(2):
            here = jnp.logical_and(diagonal, core == h)

            @pl.when(here)
            def _(h=h):
                pltpu.make_async_copy(
                    own.at[:, pl.ds(h * local_a, local_a), columns(order)],
                    mirror.at[core, :, :, columns(order)],
                    x_recv.at[order, core],
                ).start()

            @pl.when(jnp.logical_not(here))
            def _(h=h):
                swap_copy(order, h).start()

    def turn(order):
        of_chip = slab
        for bit in (1, 2):
            if order & bit:
                of_chip = of_chip + bit - 2 * bit * ((slab // bit) % 2)
        theirs = pl.ds(pl.multiple_of(of_chip * rows2, rows2), rows2)
        dot = functools.partial(lax.dot_general, dimension_numbers=NN, preferred_element_type=F32)
        for e in range(2):
            pltpu.make_async_copy(
                own.at[:, pl.ds(0, local_a), theirs],
                mirror.at[e, :, :, theirs],
                x_recv.at[order, e],
            ).wait()
            hi, lo = split2(mirror[e, :, :, theirs].reshape(local_a * local_a, rows2))
            moves = perm[theirs, :]
            got = (dot(hi, moves) + dot(lo, moves)).reshape(turned.shape[1:])
            turned[e] = got if order == 0 else turned[e] + got

    for t in range(ntile):
        widen(0, t)
    for h in range(PARTS):
        go(0, 2, 0, PARTS - 1 - h, 2, 0)
        go(0, 4, 1, h, 4, 1)
    for t in range(ntile):
        for h in range(PARTS):
            landed(1, t, h)
        widen(1, t)
    multiply(0)
    give_away(0)

    size = perm.shape[0]

    def fill_perm(i, carry):
        at = pl.ds(pl.multiple_of(i * LANES, LANES), LANES)
        row = lax.broadcasted_iota(jnp.int32, (LANES, size), 0) + i * LANES
        col = lax.broadcasted_iota(jnp.int32, (LANES, size), 1)
        perm[at, :] = jnp.where(col == (row % NO) * NO + row // NO, 1.0, 0.0).astype(BF16)
        return carry

    lax.fori_loop(0, size // LANES, fill_perm, 0)

    for h in range(PARTS):
        landed(4, 0, h)
        if h == 0:
            go(4, 6, 0, h, 2, 3)
        go(4, 5, 0, h, 1, 5)
        landed(2, 1, h)
        go(2, 3, 1, h, 1, 4)
    own[:, :, columns(0)] = slab_sum(0)
    swap(0)
    widen(2, 1)
    widen(4, 0)
    for h in range(PARTS):
        landed(3, 1, h)
        landed(5, 0, h)
    widen(3, 1)
    widen(5, 0)
    multiply(1)
    give_away(1)
    turn(0)

    for h in range(PARTS):
        back = PARTS - 1 - h
        landed(2, 0, back)
        if h == 0:
            go(2, 6, 0, back, 4, 3)
            go(2, 6, 1, back, 4, 3)
        go(2, 3, 0, back, 1, 4)
        landed(4, 1, h)
        if h == 0:
            go(4, 6, 1, h, 2, 3)
        go(4, 5, 1, h, 1, 5)
    group_sum[...] = slab_sum(1)
    widen(2, 0)
    widen(4, 1)
    for h in range(PARTS):
        landed(3, 0, h)
        landed(5, 1, h)
    widen(3, 0)
    widen(5, 1)
    multiply(2)
    give_away(2)

    for t in range(ntile):
        for h in range(PARTS):
            landed(6, t, h)
            go(6, 7, t, h, 1, 6)
        widen(6, t, True)
        for h in range(PARTS):
            landed(7, t, h)
        widen(7, t, True)
        multiply(3 + t)
        give_away(3 + t)
        if t > 0:
            continue
        early, late = group_sum[...], slab_sum(2)
        left = lax.broadcasted_iota(jnp.int32, early.shape, 2) % LANES < TILE
        own[:, :, columns(1)] = jnp.where(left, late, early)
        own[:, :, columns(2)] = jnp.where(left, early, late)
        swap(1)
        swap(2)

    turn(1)
    turn(2)
    zero, one = slab_sum(3), slab_sum(4)
    left = lax.broadcasted_iota(jnp.int32, zero.shape, 2) < TILE
    front = jnp.where(left, zero, pltpu.roll(one, TILE, 2))
    back = jnp.where(left, pltpu.roll(zero, TILE, 2), one)
    own[:, :, columns(3)] = jnp.concatenate([front, back], axis=2)
    swap(3)
    turn(3)
    for e in range(2):
        at = pl.ds(e * local_a, local_a)
        for k in range(local_a):
            out_ref[k, at, :] = own[k, at, :] + turned[e, :, k, :]

    for copy in started:
        copy.wait_send()
    for group in range(5):
        for d in range(1, nslab):
            z_copy(group, d).wait_send()
    for order in range(4):
        for h in range(2):
            @pl.when(jnp.logical_not(jnp.logical_and(diagonal, core == h)))
            def _(order=order, h=h):
                swap_copy(order, h).wait_send()


def square_shards(nslab, amplitudes, integrals, tile_mask):
    row_count, slab_cols = amplitudes.shape
    local_a, window, _ = integrals.shape
    tiles = slab_cols // TILE
    ntile = row_count // TILE
    total_rows = tile_mask.shape[0] * TILE
    most = (3 * tiles) // 4
    slots = -(-(most + 1) // (2 * PARTS)) * (2 * PARTS)
    npair = slots // 2

    mask = lax.dynamic_slice_in_dim(tile_mask, lax.axis_index("slab") * tiles, tiles, 1)
    before = jnp.triu(jnp.ones((tiles, tiles), F32), 1)
    place = jnp.dot(mask.astype(F32), before).astype(jnp.int32)
    slot = jnp.where(mask == 1, place, slots - 1)
    mine = lax.dynamic_slice_in_dim(slot, lax.axis_index("pairs") * ntile, ntile, 0)
    ids = jnp.arange(tiles, dtype=jnp.int32)
    hit = mine[:, None, :] == jnp.arange(slots, dtype=jnp.int32)[None, :, None]
    pick = jnp.max(jnp.where(hit, ids[None, None, :], 0), axis=2)

    def table(ids):
        return ids >> 1, (ids + jnp.arange(ids.shape[1], dtype=jnp.int32)) & 1


    ab = local_a * window
    rows2 = 2 * row_count
    kstep = 10 * LANES
    vcols = 5 * LANES
    vpairs = tiles // 2
    vstep = max(n for n in range(1, 6) if vpairs % n == 0)
    dims = (nslab, npair, vpairs, kstep, vstep)
    vmem = pl.BlockSpec(memory_space=pltpu.VMEM)
    smem = pl.BlockSpec(memory_space=pltpu.SMEM)
    band = window // nslab
    dma = pltpu.SemaphoreType.DMA
    return pl.pallas_call(
        functools.partial(kernel, dims),
        out_shape=jax.ShapeDtypeStruct((local_a, band, total_rows), F32),
        in_specs=[smem] * 4 + [pl.BlockSpec(memory_space=pl.ANY)] * 2,
        out_specs=vmem,
        scratch_shapes=[
            *[pltpu.VMEM((npair, TILE, LANES), F32)] * (8 * ntile),
            pltpu.VMEM((ntile, tiles // 2, TILE, LANES), F32),
            pltpu.VMEM((ab, slab_cols), BF16),
            pltpu.VMEM((ab, slab_cols), BF16),
            pltpu.VMEM((rows2, slab_cols), BF16),
            pltpu.VMEM((rows2, slab_cols), BF16),
            pltpu.VMEM((2, ab, vcols), F32),
            pltpu.VMEM((4, local_a, window, rows2), F32),
            pltpu.VMEM((4, nslab - 1, local_a, band, rows2), F32),
            pltpu.VMEM((local_a, band, rows2), F32),
            pltpu.VMEM((local_a, band, total_rows), F32),
            pltpu.VMEM((2, local_a, local_a, total_rows), F32),
            pltpu.VMEM((2, local_a, local_a, total_rows), F32),
            pltpu.VMEM((total_rows, total_rows), BF16),
            dma((ntile,)),
            dma((2,)),
            dma((7, ntile, PARTS)),
            dma((8, ntile, PARTS)),
            dma((5, nslab - 1)),
            dma((5, nslab - 1)),
            dma((4, 2)),
            dma((4, 2)),
        ],
        compiler_params=pltpu.CompilerParams(
            collective_id=0, has_side_effects=True, vmem_limit_bytes=60 * 2**20
        ),
        cost_estimate=pl.CostEstimate(
            flops=6 * ab * total_rows * slab_cols,
            bytes_accessed=4 * (ab + row_count) * slab_cols,
            transcendentals=0,
        ),
    )(*table(pick), *table(slot), amplitudes, integrals.reshape(ab, slab_cols))


def solution(mesh):
    square = mesh.shape["pairs"] == 2 * mesh.shape["slab"] == 2 * 2 * 2
    body = functools.partial(square_shards, mesh.shape["slab"]) if square else plain_shards
    return jax.shard_map(
        body,
        mesh=mesh,
        in_specs=(P("pairs", "slab"), P("pairs", None, "slab"), P()),
        out_specs=P("pairs", "slab", None),
        check_vma=False,
    )
```

```python
import functools

import jax
import jax.numpy as jnp
from jax import lax
from jax.experimental import pallas as pl
from jax.experimental.pallas import tpu as pltpu
from jax.sharding import PartitionSpec as P

MESH = pl.DeviceIdType.MESH
NO = 32
TILE = 64
LANES = 128
PARTS = 2
F32 = jnp.float32
BF16 = jnp.bfloat16
NT = (((1,), (1,)), ((), ()))
NN = (((1,), (0,)), ((), ()))


def mirrored(source, local_a, window):
    turned = source.reshape(window, local_a, NO, NO).transpose(1, 0, 3, 2)
    return turned.reshape(local_a, window, NO * NO)


def plain_shards(amplitudes, integrals, tile_mask):
    row_count, slab_cols = amplitudes.shape
    local_a, window, _ = integrals.shape
    slab_tiles = slab_cols // TILE
    mask_slab = lax.dynamic_slice_in_dim(
        tile_mask, lax.axis_index("slab") * slab_tiles, slab_tiles, 1
    )
    row_tile = (lax.axis_index("pairs") * row_count + jnp.arange(row_count, dtype=jnp.int32)) // TILE
    flat_ints = integrals.reshape(local_a * window, slab_cols)
    local_mask = jnp.take(mask_slab, row_tile, axis=0).astype(F32)
    masked = amplitudes * jnp.repeat(local_mask, TILE, axis=1)
    partial_value = lax.dot_general(
        flat_ints,
        lax.all_gather(masked, "pairs", axis=0, tiled=True),
        NT,
        precision=lax.Precision.HIGHEST,
        preferred_element_type=F32,
    )
    total_rows = partial_value.shape[1]
    partial3 = partial_value.reshape(local_a, window, total_rows)
    swapped = lax.all_to_all(partial3, "pairs", split_axis=1, concat_axis=0, tiled=True)
    combined = partial3 + mirrored(swapped, local_a, window)
    return lax.psum_scatter(combined, "slab", scatter_dimension=1, tiled=True)


def split2(x):
    hi = x.astype(BF16)
    return hi, (x - hi.astype(F32)).astype(BF16)


def join_halves(first, second, turn_first, turn_second):
    lane = lax.broadcasted_iota(jnp.int32, first.shape, 1)
    left = lane < TILE
    straight = jnp.where(left, first, second)
    swapped = pltpu.roll(jnp.where(left, second, first), TILE, 1)
    turn = jnp.where(left, jnp.full(first.shape, turn_first), jnp.full(first.shape, turn_second))
    return jnp.where(turn == 1, swapped, straight)


def kernel(
    dims, pick_ref, pick_turn, slot_ref, slot_turn, amp_ref, ints_ref, out_ref, *scratch,
):
    nslab, npair, vpairs, kstep, vstep = dims
    ntile = 2
    buf = [scratch[ntile * block : ntile * (block + 1)] for block in range(8)]
    (
        tiles_in, v_hi, v_lo, t_hi, t_lo, stage, part, zbuf, group_sum, own, mirror, turned, perm,
        amp_sem, stage_sem, send_sem, recv_sem, z_send, z_recv, x_send, x_recv,
    ) = scratch[8 * ntile :]
    pairs, slab = lax.axis_index("pairs"), lax.axis_index("slab")
    chip, core = pairs // 2, pairs % 2
    depth = npair // PARTS
    local_a, window, _ = part.shape[1:]
    band = window // nslab
    rows2 = 2 * ntile * TILE
    vcols = stage.shape[2]
    nstage = v_hi.shape[1] // vcols
    diagonal = slab == chip

    def flip(bits):
        got = pairs
        for bit in (1, 2, 4):
            if bits & bit:
                got = got + bit - 2 * bit * ((pairs // bit) % 2)
        return got

    peers = [lax.rem(slab + d, nslab) for d in range(1, nslab)]
    partners = [(2 * slab + h, chip) for h in range(2)]

    def fetch(i):
        return pltpu.make_async_copy(
            ints_ref.at[:, pl.ds(pl.multiple_of(i * vcols, LANES), vcols)],
            stage.at[lax.rem(i, 2)],
            stage_sem.at[lax.rem(i, 2)],
        )

    for t in range(ntile):
        def bring(v, carry, t=t):
            pltpu.make_async_copy(
                amp_ref.at[pl.ds(t * TILE, TILE), pl.ds(pl.multiple_of(v * LANES, LANES), LANES)],
                tiles_in.at[t, v],
                amp_sem.at[t],
            ).start()
            return carry

        lax.fori_loop(0, vpairs, bring, 0)
    fetch(0).start()

    barrier = pltpu.get_barrier_semaphore()
    for bits in (1, 2, 4):
        pl.semaphore_signal(barrier, inc=1, device_id=(flip(bits), slab), device_id_type=MESH)
    for peer in peers:
        pl.semaphore_signal(barrier, inc=1, device_id=(pairs, peer), device_id_type=MESH)

    @pl.when(jnp.logical_not(diagonal))
    def _():
        for partner in partners:
            pl.semaphore_signal(barrier, inc=1, device_id=partner, device_id_type=MESH)
        pl.semaphore_wait(barrier, 4 + nslab)

    @pl.when(diagonal)
    def _():
        pl.semaphore_wait(barrier, 2 + nslab)

    def send(src, dst, tile, piece, bits, lane):
        return pltpu.make_async_remote_copy(
            src_ref=buf[src][tile].at[pl.ds(piece * depth, depth)],
            dst_ref=buf[dst][tile].at[pl.ds(piece * depth, depth)],
            send_sem=send_sem.at[lane, tile, piece],
            recv_sem=recv_sem.at[dst, tile, piece],
            device_id=(flip(bits), slab),
            device_id_type=MESH,
        )

    started = []

    def go(*args):
        copy = send(*args)
        copy.start()
        started.append(copy)

    def landed(block, tile, piece):
        send(0, block, tile, piece, 1, 0).wait_recv()

    for t in range(ntile):
        pltpu.make_async_copy(tiles_in.at[t], tiles_in.at[t], amp_sem.at[t]).wait()
    for h in range(PARTS):
        for t in range(ntile):
            def pack(j, carry, t=t, h=h):
                w = h * depth + j
                joined = join_halves(
                    tiles_in[t, pick_ref[t, 2 * w]], tiles_in[t, pick_ref[t, 2 * w + 1]],
                    pick_turn[t, 2 * w], pick_turn[t, 2 * w + 1],
                )
                lane = lax.broadcasted_iota(jnp.int32, joined.shape, 1)
                last = jnp.full(joined.shape, w) == npair - 1
                buf[0][t][w] = jnp.where(jnp.logical_and(lane >= TILE, last), 0.0, joined)
                return carry

            lax.fori_loop(0, depth, pack, 0)
            if t == 0:
                go(0, 4, t, h, 4, 1)
            else:
                go(0, 2, t, h, 2, 0)
            go(0, 1, t, h, 1, 2)

    def split_ints(i, carry):
        @pl.when(i + 1 < nstage)
        def _():
            fetch(i + 1).start()

        fetch(i).wait()
        at = pl.ds(pl.multiple_of(i * vcols, LANES), vcols)
        hi, lo = split2(stage[lax.rem(i, 2)])
        v_hi[:, at] = hi
        v_lo[:, at] = lo
        return carry

    lax.fori_loop(0, nstage, split_ints, 0)

    def chip_of(order):
        return flip(2 * order) // 2

    def widen(block, t, by_tile=False):
        device = flip(block)
        row_tile = device * ntile + t
        spot = 2 * t + device % 2 if by_tile else (device % 2) * ntile + t
        rows = pl.ds(pl.multiple_of(spot * TILE, TILE), TILE)
        source = buf[block][t]

        def some(i, carry):
            made = []
            for j in range(vstep):
                v = i * vstep + j
                joined = join_halves(
                    source[slot_ref[row_tile, 2 * v]], source[slot_ref[row_tile, 2 * v + 1]],
                    slot_turn[row_tile, 2 * v], slot_turn[row_tile, 2 * v + 1],
                )
                made.append(split2(joined))
            at = pl.ds(pl.multiple_of(i * (vstep * LANES), LANES), vstep * LANES)
            t_hi[rows, at] = jnp.concatenate([hi for hi, _ in made], axis=1)
            t_lo[rows, at] = jnp.concatenate([lo for _, lo in made], axis=1)
            return carry

        lax.fori_loop(0, vpairs // vstep, some, 0)

    def extent(group):
        if group < 3:
            return group, pl.ds(0, rows2)
        return 3, pl.ds((group - 3) * LANES, LANES)

    def multiply(group):
        at_part, rows = extent(group)
        part[at_part, :, :, rows] = jnp.zeros((local_a, window, rows.size), F32)

        def step(k, carry):
            at = pl.ds(pl.multiple_of(k * kstep, LANES), kstep)
            dot = functools.partial(lax.dot_general, dimension_numbers=NT, preferred_element_type=F32)
            vh, vl, th, tl = v_hi[:, at], v_lo[:, at], t_hi[rows, at], t_lo[rows, at]
            total = dot(vh, th) + dot(vh, tl) + dot(vl, th)
            part[at_part, :, :, rows] += total.reshape(local_a, window, rows.size)
            return carry

        lax.fori_loop(0, t_hi.shape[1] // kstep, step, 0)

    def z_copy(group, d):
        at_part, rows = extent(group)
        return pltpu.make_async_remote_copy(
            src_ref=part.at[at_part, :, pl.ds(pl.multiple_of(peers[d - 1] * band, band), band), rows],
            dst_ref=zbuf.at[at_part, d - 1, :, :, rows],
            send_sem=z_send.at[group, d - 1],
            recv_sem=z_recv.at[group, d - 1],
            device_id=(pairs, peers[d - 1]),
            device_id_type=MESH,
        )

    def give_away(group):
        for d in range(1, nslab):
            z_copy(group, d).start()

    def slab_sum(group):
        at_part, rows = extent(group)
        for d in range(1, nslab):
            z_copy(group, d).wait_recv()
        total = part[at_part, :, pl.ds(pl.multiple_of(slab * band, band), band), rows]
        for d in range(1, nslab):
            total = total + zbuf[at_part, d - 1, :, :, rows]
        return total

    def columns(order):
        return pl.ds(pl.multiple_of(chip_of(order) * rows2, rows2), rows2)

    def swap_copy(order, h):
        return pltpu.make_async_remote_copy(
            src_ref=own.at[:, pl.ds(h * local_a, local_a), columns(order)],
            dst_ref=mirror.at[core, :, :, columns(order)],
            send_sem=x_send.at[order, h],
            recv_sem=x_recv.at[order, core],
            device_id=partners[h],
            device_id_type=MESH,
        )

    def swap(order):
        for h in range(2):
            here = jnp.logical_and(diagonal, core == h)

            @pl.when(here)
            def _(h=h):
                pltpu.make_async_copy(
                    own.at[:, pl.ds(h * local_a, local_a), columns(order)],
                    mirror.at[core, :, :, columns(order)],
                    x_recv.at[order, core],
                ).start()

            @pl.when(jnp.logical_not(here))
            def _(h=h):
                swap_copy(order, h).start()

    def turn(order):
        of_chip = slab
        for bit in (1, 2):
            if order & bit:
                of_chip = of_chip + bit - 2 * bit * ((slab // bit) % 2)
        theirs = pl.ds(pl.multiple_of(of_chip * rows2, rows2), rows2)
        dot = functools.partial(lax.dot_general, dimension_numbers=NN, preferred_element_type=F32)
        for e in range(2):
            pltpu.make_async_copy(
                own.at[:, pl.ds(0, local_a), theirs],
                mirror.at[e, :, :, theirs],
                x_recv.at[order, e],
            ).wait()
            hi, lo = split2(mirror[e, :, :, theirs].reshape(local_a * local_a, rows2))
            moves = perm[theirs, :]
            got = (dot(hi, moves) + dot(lo, moves)).reshape(turned.shape[1:])
            turned[e] = got if order == 0 else turned[e] + got

    for t in range(ntile):
        widen(0, t)
    for h in range(PARTS):
        go(0, 2, 0, PARTS - 1 - h, 2, 0)
        go(0, 4, 1, h, 4, 1)
    for t in range(ntile):
        for h in range(PARTS):
            landed(1, t, h)
        widen(1, t)
    multiply(0)
    give_away(0)

    size = perm.shape[0]

    def fill_perm(i, carry):
        at = pl.ds(pl.multiple_of(i * LANES, LANES), LANES)
        row = lax.broadcasted_iota(jnp.int32, (LANES, size), 0) + i * LANES
        col = lax.broadcasted_iota(jnp.int32, (LANES, size), 1)
        perm[at, :] = jnp.where(col == (row % NO) * NO + row // NO, 1.0, 0.0).astype(BF16)
        return carry

    lax.fori_loop(0, size // LANES, fill_perm, 0)

    for h in range(PARTS):
        landed(4, 0, h)
        if h == 0:
            go(4, 6, 0, h, 2, 3)
        go(4, 5, 0, h, 1, 5)
        landed(2, 1, h)
        go(2, 3, 1, h, 1, 4)
    own[:, :, columns(0)] = slab_sum(0)
    swap(0)
    widen(2, 1)
    widen(4, 0)
    for h in range(PARTS):
        landed(3, 1, h)
        landed(5, 0, h)
    widen(3, 1)
    widen(5, 0)
    multiply(1)
    give_away(1)
    turn(0)

    for h in range(PARTS):
        back = PARTS - 1 - h
        landed(2, 0, back)
        if h == 0:
            go(2, 6, 0, back, 4, 3)
            go(2, 6, 1, back, 4, 3)
        go(2, 3, 0, back, 1, 4)
        landed(4, 1, h)
        if h == 0:
            go(4, 6, 1, h, 2, 3)
        go(4, 5, 1, h, 1, 5)
    group_sum[...] = slab_sum(1)
    widen(2, 0)
    widen(4, 1)
    for h in range(PARTS):
        landed(3, 0, h)
        landed(5, 1, h)
    widen(3, 0)
    widen(5, 1)
    multiply(2)
    give_away(2)

    for t in range(ntile):
        for h in range(PARTS):
            landed(6, t, h)
            go(6, 7, t, h, 1, 6)
        widen(6, t, True)
        for h in range(PARTS):
            landed(7, t, h)
        widen(7, t, True)
        multiply(3 + t)
        give_away(3 + t)
        if t > 0:
            continue
        early, late = group_sum[...], slab_sum(2)
        left = lax.broadcasted_iota(jnp.int32, early.shape, 2) % LANES < TILE
        own[:, :, columns(1)] = jnp.where(left, late, early)
        own[:, :, columns(2)] = jnp.where(left, early, late)
        swap(1)
        swap(2)

    turn(1)
    turn(2)
    zero, one = slab_sum(3), slab_sum(4)
    left = lax.broadcasted_iota(jnp.int32, zero.shape, 2) < TILE
    front = jnp.where(left, zero, pltpu.roll(one, TILE, 2))
    back = jnp.where(left, pltpu.roll(zero, TILE, 2), one)
    own[:, :, columns(3)] = jnp.concatenate([front, back], axis=2)
    swap(3)
    turn(3)
    for e in range(2):
        at = pl.ds(e * local_a, local_a)
        for k in range(local_a):
            out_ref[k, at, :] = own[k, at, :] + turned[e, :, k, :]

    for copy in started:
        copy.wait_send()
    for group in range(5):
        for d in range(1, nslab):
            z_copy(group, d).wait_send()
    for order in range(4):
        for h in range(2):
            @pl.when(jnp.logical_not(jnp.logical_and(diagonal, core == h)))
            def _(order=order, h=h):
                swap_copy(order, h).wait_send()


def square_shards(nslab, amplitudes, integrals, tile_mask):
    row_count, slab_cols = amplitudes.shape
    local_a, window, _ = integrals.shape
    tiles = slab_cols // TILE
    ntile = row_count // TILE
    total_rows = tile_mask.shape[0] * TILE
    most = (3 * tiles) // 4
    slots = -(-(most + 1) // (2 * PARTS)) * (2 * PARTS)
    npair = slots // 2

    mask = lax.dynamic_slice_in_dim(tile_mask, lax.axis_index("slab") * tiles, tiles, 1)
    before = jnp.triu(jnp.ones((tiles, tiles), F32), 1)
    place = jnp.dot(mask.astype(F32), before).astype(jnp.int32)
    slot = jnp.where(mask == 1, place, slots - 1)
    mine = lax.dynamic_slice_in_dim(slot, lax.axis_index("pairs") * ntile, ntile, 0)
    ids = jnp.arange(tiles, dtype=jnp.int32)
    hit = mine[:, None, :] == jnp.arange(slots, dtype=jnp.int32)[None, :, None]
    pick = jnp.max(jnp.where(hit, ids[None, None, :], 0), axis=2)

    def table(ids):
        return ids >> 1, (ids + jnp.arange(ids.shape[1], dtype=jnp.int32)) & 1


    ab = local_a * window
    rows2 = 2 * row_count
    kstep = 10 * LANES
    vcols = 5 * LANES
    vpairs = tiles // 2
    vstep = max(n for n in range(1, 11) if vpairs % n == 0)
    dims = (nslab, npair, vpairs, kstep, vstep)
    vmem = pl.BlockSpec(memory_space=pltpu.VMEM)
    smem = pl.BlockSpec(memory_space=pltpu.SMEM)
    band = window // nslab
    dma = pltpu.SemaphoreType.DMA
    return pl.pallas_call(
        functools.partial(kernel, dims),
        out_shape=jax.ShapeDtypeStruct((local_a, band, total_rows), F32),
        in_specs=[smem] * 4 + [pl.BlockSpec(memory_space=pl.ANY)] * 2,
        out_specs=vmem,
        scratch_shapes=[
            *[pltpu.VMEM((npair, TILE, LANES), F32)] * (8 * ntile),
            pltpu.VMEM((ntile, tiles // 2, TILE, LANES), F32),
            pltpu.VMEM((ab, slab_cols), BF16),
            pltpu.VMEM((ab, slab_cols), BF16),
            pltpu.VMEM((rows2, slab_cols), BF16),
            pltpu.VMEM((rows2, slab_cols), BF16),
            pltpu.VMEM((2, ab, vcols), F32),
            pltpu.VMEM((4, local_a, window, rows2), F32),
            pltpu.VMEM((4, nslab - 1, local_a, band, rows2), F32),
            pltpu.VMEM((local_a, band, rows2), F32),
            pltpu.VMEM((local_a, band, total_rows), F32),
            pltpu.VMEM((2, local_a, local_a, total_rows), F32),
            pltpu.VMEM((2, local_a, local_a, total_rows), F32),
            pltpu.VMEM((total_rows, total_rows), BF16),
            dma((ntile,)),
            dma((2,)),
            dma((7, ntile, PARTS)),
            dma((8, ntile, PARTS)),
            dma((5, nslab - 1)),
            dma((5, nslab - 1)),
            dma((4, 2)),
            dma((4, 2)),
        ],
        compiler_params=pltpu.CompilerParams(
            collective_id=0, has_side_effects=True, vmem_limit_bytes=60 * 2**20
        ),
        cost_estimate=pl.CostEstimate(
            flops=6 * ab * total_rows * slab_cols,
            bytes_accessed=4 * (ab + row_count) * slab_cols,
            transcendentals=0,
        ),
    )(*table(pick), *table(slot), amplitudes, integrals.reshape(ab, slab_cols))


def solution(mesh):
    square = mesh.shape["pairs"] == 2 * mesh.shape["slab"] == 2 * 2 * 2
    body = functools.partial(square_shards, mesh.shape["slab"]) if square else plain_shards
    return jax.shard_map(
        body,
        mesh=mesh,
        in_specs=(P("pairs", "slab"), P("pairs", None, "slab"), P()),
        out_specs=P("pairs", "slab", None),
        check_vma=False,
    )
```
